256 devices in a mesh: query: 8 (over z), doc: 16 (over x, y), tok: 2 (over core).
Axes of the slice: x: 4, y: 4, z: 8, core: 2. Of those that a mesh axis runs over, the one named last changes fastest.
Arguments:
- queries: bfloat16 [2048, 32, 128], P(('query', 'doc'), 'tok'), may hold values from -14 to 14
- documents: bfloat16 [512, 128, 128], P(('query', 'doc')), may hold values from -14 to 14
- doc_lengths: int32 [512], P(('query', 'doc')), may hold values from 1 to 128, 40960 in all
- candidates: int32 [256, 256], P(('query', 'doc')), may hold values from 0 to 511, all different within a row
Outputs:
- top_scores: float32 [2048, 128], P(('query', 'doc'))
The draws below stay inside these ranges and needn't reach their ends.
Inputs may be any that keep to these rules, and one draw needn't show every extreme that they name: `candidates`: each row names 256 different document block ids; every id appears in some row. `doc_lengths`: the counts sum to 40960.
All inputs are finite; a program needn't handle non-finite values. No bound on the sum of `doc_lengths` on one device may be relied on, other than what follows from the above.
Results may differ from the reference program's by a relative error of at most 0.0003.
Values may be sent and summed in bfloat16 or wider, within the bound.
A program may use at most 64 MiB of HBM per device.

```python
import math
import jax
import jax.numpy as jnp
import numpy as np
from jax import lax

DIM = 128
QTOK = 32
DTOK = 128
QBLK = 8
QUERIES = 2048
DOCS = 512
QBLOCKS = 256
CAND = 256
TOPK = 128


def query_field(key):
    inner_key = jax.random.fold_in(key, 7101)
    shape_all = (QUERIES, QTOK, DIM)
    base_values = jax.random.normal(inner_key, shape_all, jnp.float32)
    return jnp.clip(base_values, -6.0, 6.0)


def draw_queries(key, part):
    source = query_field(key)
    return source.astype(jnp.bfloat16)


def draw_documents(key, part):
    source = query_field(key)
    doc_key = jax.random.fold_in(key, 7202)
    block_key = jax.random.fold_in(doc_key, 1)
    member_key = jax.random.fold_in(doc_key, 2)
    token_key = jax.random.fold_in(doc_key, 3)
    weight_key = jax.random.fold_in(doc_key, 4)
    noise_key = jax.random.fold_in(doc_key, 5)
    blocks = jax.random.randint(block_key, (DOCS, 1), 0, QBLOCKS)
    members = jax.random.randint(member_key, (DOCS, DTOK), 0, QBLK)
    tokens = jax.random.randint(token_key, (DOCS, DTOK), 0, QTOK)
    query_index = (blocks * QBLK + members).astype(jnp.int32)
    copied = source[query_index, tokens.astype(jnp.int32)]
    weight_mix = jax.random.uniform(weight_key, (DOCS, 1, 1), jnp.float32, 0.0, 1.0)
    noise_part = jnp.clip(jax.random.normal(noise_key, (DOCS, DTOK, DIM), jnp.float32), -6.0, 6.0)
    mixed = weight_mix * copied + (1.0 - weight_mix) * noise_part
    return mixed.astype(jnp.bfloat16)


def choose_distinct(rng, rows, number_of, top, lift):
    order = jax.random.permutation(jax.random.fold_in(rng, 1), number_of)
    boost = order
    for power in range(3):
        boost = boost * boost // number_of
    boost = boost * lift // number_of
    tickets = jax.random.randint(jax.random.fold_in(rng, 2), (rows, number_of), 0, 4096) + boost
    sure = jax.random.permutation(jax.random.fold_in(rng, 3), rows)[jnp.arange(number_of) % rows]
    tickets = jnp.where(jnp.arange(rows)[:, None] == sure[None, :], 1 << 14, tickets)
    score = tickets * number_of + jnp.arange(number_of)
    return lax.top_k(score.astype(jnp.int32), top)[1].astype(jnp.int32)


def profile(count, total, limit, slope):
    loads = [(1 << 20) // math.isqrt(standing ** slope) + 1 for standing in range(2, count + 1)]
    rest, counts = total - limit - (count - 1), [1] * (count - 1)
    while rest > 0:
        free = [i for i in range(count - 1) if counts[i] < limit]
        pool, budget = sum([loads[i] for i in free]), rest
        for i in free:
            addition = min(limit - counts[i], max(1, budget * loads[i] // pool), rest)
            counts[i] = counts[i] + addition
            rest = rest - addition
    return np.array([limit] + counts)


def uneven_parts(key, count, total, reach, skew):
    if count == 2:
        one = jax.random.randint(key, (), max(1, total - reach), min(reach, total - 1) + 1)
        return jnp.stack([one, total - one])
    sizes = jnp.asarray(profile(count, total, reach, skew), jnp.int32)
    pairs = (count - 1) // 2
    donor, sink = sizes[1:1 + 2 * pairs:2], sizes[2:2 + 2 * pairs:2]
    slack = jnp.minimum(donor - 1, reach - sink)
    moved = jax.random.randint(jax.random.fold_in(key, 1), (pairs,), 0, 1 << 20) % (slack + 1)
    sizes = sizes.at[1:1 + 2 * pairs:2].set(donor - moved).at[2:2 + 2 * pairs:2].set(sink + moved)
    return sizes[jax.random.permutation(jax.random.fold_in(key, 2), count)]


def setup_inputs(seed: int = 0) -> dict:
    keys = jax.random.split(jax.random.key(seed), 5)
    return {
        "queries": draw_queries(jax.random.fold_in(keys[4], 71), 0),
        "documents": draw_documents(jax.random.fold_in(keys[4], 71), 0),
        "doc_lengths": uneven_parts(keys[2], DOCS, DOCS * DTOK * 5 // 8, DTOK, 2).astype(jnp.int32),
        "candidates": choose_distinct(keys[3], QBLOCKS, DOCS, CAND, 8192),
    }


epsilon = 1e-06
absent_score = -10000.0
excluded_score = -1e+30

def unit_rows(values):
    widened = values.astype(jnp.float32)
    scale = lax.rsqrt(lax.optimization_barrier(jnp.sum(widened * widened, axis=-1, keepdims=True)) + epsilon)
    return (widened * scale).astype(jnp.bfloat16)

def block_size(doc_count):
    if doc_count % 4 == 0:
        return 4
    if doc_count % 2 == 0:
        return 2
    return 1

def maxsim(query_rows, docs, lengths):
    doc_count = docs.shape[0]
    block_width = block_size(doc_count)
    row_count = query_rows.shape[0]
    query_tokens = query_rows.shape[1]
    flat_queries = query_rows.reshape(row_count * query_tokens, query_rows.shape[2])
    doc_tokens = docs.shape[1]
    blocked_docs = docs.reshape(doc_count // block_width, block_width * doc_tokens, docs.shape[2])
    blocked_lengths = lengths.reshape(doc_count // block_width, block_width)
    positions = jnp.arange(doc_tokens, dtype=jnp.int32)

    def one_block(operands):
        block_docs, block_lengths = operands
        similar = lax.dot_general(flat_queries, block_docs, (((1,), (1,)), ((), ())), preferred_element_type=jnp.float32)
        similar = similar.reshape(row_count, query_tokens, block_width, doc_tokens)
        live_mask = positions[None, :] < block_lengths[:, None]
        similar = jnp.where(live_mask[None, None], similar, absent_score)
        return lax.optimization_barrier(jnp.sum(lax.optimization_barrier(jnp.max(similar, axis=3)), axis=1)).T
    return lax.map(one_block, (blocked_docs, blocked_lengths)).reshape(doc_count, row_count)

def rank_rows(row_scores, lists, doc_ids, keep_count):
    live_mask = jnp.any(lists[:, :, None] == doc_ids[None, None, :], axis=1)
    live_mask = jnp.repeat(live_mask, QBLK, axis=0)
    masked = jnp.where(live_mask, row_scores, excluded_score)
    if masked.shape[1] < keep_count:
        padding = jnp.full((masked.shape[0], keep_count - masked.shape[1]), excluded_score, jnp.float32)
        masked = jnp.concatenate([masked, padding], axis=1)
    return lax.top_k(masked, keep_count)[0]

def reference(queries, documents, doc_lengths, candidates):
    query_unit = unit_rows(queries)
    doc_unit = unit_rows(documents)
    scores = maxsim(query_unit, doc_unit, doc_lengths)
    doc_ids = jnp.arange(DOCS, dtype=jnp.int32)
    return rank_rows(scores.T, candidates, doc_ids, TOPK)
```

```python
import jax
import jax.numpy as jnp
from jax import lax
from jax.experimental import pallas as pl
from jax.experimental.pallas import tpu as pltpu
from jax.sharding import PartitionSpec as P

MESH = pl.DeviceIdType.MESH
epsilon = 1e-06
excluded_score = -1e30

OWN, UP1, DN1, UP2, DN2, UP3, DN3, FAR = range(8)
ZOFF = (0, 7, 2, 5, 1, 6, 3, 4)


def unit_rows(values):
    widened = values.astype(jnp.float32)
    return widened * lax.rsqrt(jnp.sum(widened * widened, axis=-1, keepdims=True) + epsilon)


def kernel(
    q_ref, d_ref, len_ref, cand_ref, o_ref,
    qstage, dstage, qbuf, dbuf, peaks, outbox, inbox, live, ranked,
    qsend, qrecv, dsend, drecv, csend, crecv, ssend, srecv,
):
    z = lax.axis_index("query")
    xy = lax.axis_index("doc")
    c = lax.axis_index("tok")
    x, y = xy // 4, xy % 4
    other = 1 - c

    def chip(dx, dy):
        return ((x + dx) % 4) * 4 + (y + dy) % 4

    barrier = pltpu.get_barrier_semaphore()

    def greet(n, carry):
        for tok in (0, 1):
            pl.semaphore_signal(
                barrier, inc=1, device_id={"doc": (xy + n) % 16, "tok": tok}, device_id_type=MESH
            )
        return carry

    for dz in (1, 7):
        pl.semaphore_signal(barrier, inc=1, device_id={"query": (z + dz) % 8}, device_id_type=MESH)
    pl.semaphore_signal(barrier, inc=1, device_id={"tok": other}, device_id_type=MESH)
    lax.fori_loop(1, 16, greet, 0)

    unit = unit_rows(q_ref[...]).reshape(256, 128)
    for n in range(16):
        qstage[pl.ds(n, 16, stride=16), :] = unit[n * 16:(n + 1) * 16]
    qbuf[0] = qstage[...].astype(jnp.bfloat16).reshape(2, 128, 128)
    slots = lax.broadcasted_iota(jnp.int32, (128, 128), 0)
    for w in range(4):
        unit = unit_rows(d_ref[w])
        unit = jnp.where(slots < len_ref[w], unit, unit[0:1])
        dstage[pl.ds(w, 128, stride=4), :] = unit
    dbuf[0] = dstage[...].astype(jnp.bfloat16).reshape(2, 256, 128)

    pl.semaphore_wait(barrier, 33)

    pending = []

    def q_copy(src, dst, sem, dx, dy):
        n = len([p for p in pending if p[0] == "q"])
        copy = pltpu.make_async_remote_copy(
            src_ref=src, dst_ref=dst, send_sem=qsend.at[n], recv_sem=sem,
            device_id={"doc": chip(dx, dy)}, device_id_type=MESH,
        )
        copy.start()
        pending.append(("q", copy))

    def q_whole(src, dst, dx, dy):
        q_copy(qbuf.at[src], qbuf.at[dst], qrecv.at[dst, 0], dx, dy)

    def q_half(h, src, dst, dx, dy):
        q_copy(qbuf.at[src, h], qbuf.at[dst, h], qrecv.at[dst, h], dx, dy)

    def q_wait(slot, h=None):
        ref = qbuf.at[slot] if h is None else qbuf.at[slot, h]
        pltpu.make_async_remote_copy(
            src_ref=ref, dst_ref=ref, send_sem=qsend.at[0], recv_sem=qrecv.at[slot, 0 if h is None else h],
            device_id={"doc": xy}, device_id_type=MESH,
        ).wait_recv()

    def z_copy(src, dst, part, dz):
        n = len([p for p in pending if p[0] == "d"])
        rows = pl.ds(0, 256) if part is None else pl.ds(part * 128, 128)
        copy = pltpu.make_async_remote_copy(
            src_ref=dbuf.at[src, c, rows], dst_ref=dbuf.at[dst, c, rows],
            send_sem=dsend.at[n], recv_sem=drecv.at[dst, 0 if part is None else part],
            device_id={"query": (z + dz) % 8}, device_id_type=MESH,
        )
        copy.start()
        pending.append(("d", copy))

    def z_wait(chunk, part=None):
        rows = pl.ds(0, 256) if part is None else pl.ds(part * 128, 128)
        ref = dbuf.at[chunk, c, rows]
        pltpu.make_async_remote_copy(
            src_ref=ref, dst_ref=ref, send_sem=dsend.at[0], recv_sem=drecv.at[chunk, 0 if part is None else part],
            device_id={"query": z}, device_id_type=MESH,
        ).wait_recv()

    def share(chunk):
        copy = pltpu.make_async_remote_copy(
            src_ref=dbuf.at[chunk, c], dst_ref=dbuf.at[chunk, c], send_sem=csend.at[chunk],
            recv_sem=crecv.at[chunk], device_id={"tok": other}, device_id_type=MESH,
        )
        copy.start()
        pending.append(("c", copy))

    def share_wait(chunk):
        ref = dbuf.at[chunk, other]
        pltpu.make_async_remote_copy(
            src_ref=ref, dst_ref=ref, send_sem=csend.at[0], recv_sem=crecv.at[chunk],
            device_id={"tok": c}, device_id_type=MESH,
        ).wait_recv()

    def match(slot, chunks):
        tokens = qbuf[slot].reshape(256, 128)
        for k in chunks:
            similar = lax.dot_general(
                dbuf[k].reshape(512, 128), tokens, (((1,), (1,)), ((), ())),
                preferred_element_type=jnp.float32,
            )
            peaks[slot, k] = jnp.max(similar.reshape(64, 8, 256), axis=0)

    sub = lax.broadcasted_iota(jnp.int32, (8, 128), 0)
    lane = lax.broadcasted_iota(jnp.int32, (8, 128), 1)

    def total(slot):
        pairs = []
        for p in range(4):
            both = 0.0
            for h in range(2):
                a = peaks[slot, 2 * p, :, h * 128:(h + 1) * 128]
                b = peaks[slot, 2 * p + 1, :, h * 128:(h + 1) * 128]
                first = jnp.where(sub < 4, a, b)
                second = jnp.where(sub < 4, b, a)
                both = both + jnp.maximum(first, pltpu.roll(second, 4, 0))
            pairs.append(both)
        low = lane < 64
        folded = []
        for p in (0, 2):
            a, b = pairs[p], pairs[p + 1]
            folded.append(jnp.where(low, a, b) + pltpu.roll(jnp.where(low, b, a), 64, 1))
        f0, f1 = folded
        quarter = jnp.where(lane % 64 < 32, f0 + pltpu.roll(f0, 96, 1), f1 + pltpu.roll(f1, 32, 1))
        even = quarter + pltpu.roll(quarter, 112, 1)
        odd = quarter + pltpu.roll(quarter, 16, 1)
        return jnp.where(lane % 32 < 16, even, pltpu.roll(odd, 4, 0))[0:4]

    def score_copy(slot, tok):
        return pltpu.make_async_remote_copy(
            src_ref=outbox.at[slot], dst_ref=inbox.at[c, slot], send_sem=ssend.at[slot, tok],
            recv_sem=srecv.at[c, slot],
            device_id={"doc": ((x - slot // 4 + 4) % 4) * 4 + (y - slot % 4 + 4) % 4, "tok": tok},
            device_id_type=MESH,
        )

    def deliver(slot):
        outbox[slot] = total(slot)
        score_copy(slot, 0).start()
        score_copy(slot, 1).start()

    q_whole(0, 4, 1, 0)
    q_whole(0, 12, 3, 0)
    q_whole(0, 1, 0, 1)
    q_whole(0, 3, 0, 3)
    z_copy(OWN, UP1, None, 1)
    z_copy(OWN, DN1, None, 7)

    rows = lax.broadcasted_iota(jnp.int32, (64, 256), 0)
    source = rows // 4
    row_id = (((x + source // 4) % 4) * 4 + (y + source % 4) % 4) * 4 + rows % 4
    lanes = lax.broadcasted_iota(jnp.int32, (128, 256), 0)
    group = lanes // 16
    plane = jnp.zeros_like(group)
    for g in range(8):
        plane = jnp.where(group == g, (z + ZOFF[g]) % 8, plane)
    first = cand_ref[0:1, :]
    second = cand_ref[1:2, :]
    listed = jnp.where(lanes % 16 < 8, first, second)
    by_plane = jnp.where(listed // 64 == plane, 1.0, 0.0).astype(jnp.bfloat16)
    found = []
    for block in (first, second):
        by_row = jnp.where(block % 64 == row_id, 1.0, 0.0).astype(jnp.bfloat16)
        found.append(lax.dot_general(
            by_row, by_plane, (((1,), (1,)), ((), ())), preferred_element_type=jnp.float32))
    wide_lane = lax.broadcasted_iota(jnp.int32, (64, 128), 1)
    live[...] = jnp.where(wide_lane % 16 < 8, found[0], found[1])

    match(0, (OWN,))

    near = (4, 12, 1, 3)
    q_wait(4)
    q_whole(4, 8, 1, 0)
    q_half(0, 4, 5, 0, 1)
    q_half(0, 4, 7, 0, 3)
    q_wait(12)
    q_half(0, 12, 13, 0, 1)
    q_half(0, 12, 15, 0, 3)
    q_wait(1)
    q_half(1, 1, 5, 1, 0)
    q_half(1, 1, 13, 3, 0)
    q_wait(3)
    q_whole(3, 2, 0, 3)
    q_half(1, 3, 7, 1, 0)
    q_half(1, 3, 15, 3, 0)
    z_wait(UP1)
    z_copy(UP1, UP2, None, 1)
    share(UP1)
    z_wait(DN1)
    z_copy(DN1, DN2, None, 7)
    share(DN1)

    for s in near:
        match(s, (OWN,))
    share_wait(UP1)
    share_wait(DN1)
    for s in (0,) + near:
        match(s, (UP1, DN1))

    q_wait(8)
    q_half(0, 8, 9, 0, 1)
    q_half(0, 8, 11, 0, 3)
    q_wait(2)
    q_half(1, 2, 6, 1, 0)
    q_half(1, 2, 14, 3, 0)
    for s in (5, 15, 7, 13):
        q_wait(s, 0)
        q_wait(s, 1)
    q_half(1, 5, 9, 1, 0)
    q_half(0, 5, 6, 0, 1)
    q_half(0, 15, 14, 0, 3)
    q_half(1, 15, 11, 3, 0)
    z_wait(UP2)
    z_copy(UP2, UP3, None, 1)
    share(UP2)
    z_wait(DN2)
    z_copy(DN2, DN3, None, 7)
    share(DN2)

    middle = (8, 2, 5, 7, 13, 15)
    for s in middle:
        match(s, (OWN, UP1, DN1))

    q_wait(9, 0)
    q_half(0, 9, 10, 0, 1)
    q_wait(14, 1)
    q_half(1, 14, 10, 3, 0)
    share_wait(UP2)
    share_wait(DN2)
    z_wait(UP3)
    z_copy(UP3, FAR, 0, 1)
    share(UP3)
    z_wait(DN3)
    z_copy(DN3, FAR, 1, 7)
    share(DN3)

    for s in (0,) + near + middle:
        match(s, (UP2, DN2))

    q_wait(9, 1)
    q_wait(14, 0)
    q_wait(6, 0)
    q_wait(6, 1)
    q_wait(11, 0)
    q_wait(11, 1)
    z_wait(FAR, 0)
    z_wait(FAR, 1)
    share(FAR)
    share_wait(UP3)
    share_wait(DN3)
    q_wait(10, 0)
    q_wait(10, 1)
    for s in (9, 14, 6, 11, 10):
        match(s, (OWN, UP1, DN1, UP2, DN2))
    share_wait(FAR)

    def last(n, carry):
        base = 12 - 4 * n
        for s in range(4):
            match(base + s, (UP3, DN3, FAR))
        for s in range(4):
            deliver(base + s)
        return carry

    lax.fori_loop(0, 3, last, 0)
    for s in range(4):
        match(s, (UP3, DN3, FAR))
    for s in (1, 2, 3):
        deliver(s)
    own = total(0)
    outbox[0] = own
    inbox[c, 0] = own
    sibling = pltpu.make_async_remote_copy(
        src_ref=outbox.at[0], dst_ref=inbox.at[c, 0], send_sem=ssend.at[0, 0], recv_sem=srecv.at[c, 0],
        device_id={"tok": other}, device_id_type=MESH,
    )
    sibling.start()

    for _, copy in pending:
        copy.wait_send()

    def arrive(tok, slot):
        ref = inbox.at[tok, slot]
        pltpu.make_async_remote_copy(
            src_ref=ref, dst_ref=ref, send_sem=ssend.at[0, 0], recv_sem=srecv.at[tok, slot],
            device_id={"tok": other}, device_id_type=MESH,
        ).wait_recv()

    def settle(slot, carry):
        arrive(0, slot)
        arrive(1, slot)
        score_copy(slot, 0).wait_send()
        score_copy(slot, 1).wait_send()
        return carry

    lax.fori_loop(1, 16, settle, 0)
    arrive(other, 0)
    sibling.wait_send()

    regs = []
    for v in range(8):
        pieces = [inbox[0, 2 * v + h] + inbox[1, 2 * v + h] for h in (0, 1)]
        value = jnp.concatenate(pieces, axis=0)
        regs.append(jnp.where(live[v * 8:(v + 1) * 8] > 0.0, value, excluded_score))

    def bit(k):
        return (sub >> (k - 3)) & 1 if k < 6 else (lane >> (k - 2)) & 1

    def partner(value, k):
        if k < 6:
            axis, step, size = 0, 1 << (k - 3), 8
        else:
            axis, step, size = 1, 1 << (k - 2), 128
        if 2 * step == size:
            return pltpu.roll(value, step, axis)
        return jnp.where(bit(k) == 0, pltpu.roll(value, size - step, axis), pltpu.roll(value, step, axis))

    def exchange(regs, k, flips=None):
        if k < 3:
            out = list(regs)
            for v in range(8):
                if v & (1 << k):
                    continue
                u = v | (1 << k)
                high, low = jnp.maximum(regs[v], regs[u]), jnp.minimum(regs[v], regs[u])
                if flips is not None and v & (1 << flips):
                    high, low = low, high
                out[v], out[u] = high, low
            return out
        keep_high = bit(k) == 0
        out = []
        for r in regs:
            mate = partner(r, k)
            out.append(jnp.where(keep_high, jnp.maximum(r, mate), jnp.minimum(r, mate)))
        return out

    def signed(regs, k):
        return [jnp.where(bit(k) == 0, r, -r) for r in regs]

    for phase in range(1, 10):
        top = min(phase - 1, 6)
        if phase in (8, 9):
            regs = [jnp.maximum(r, partner(r, phase - 1)) for r in regs]
        by_mask = 3 <= phase < 9
        if by_mask:
            regs = signed(regs, phase)
        for k in range(top, -1, -1):
            regs = exchange(regs, k, phase if phase < 3 else None)
        if by_mask:
            regs = signed(regs, phase)

    for v in range(8):
        ranked[pl.ds(v, 8, stride=8), :] = regs[v]
    turned = jnp.concatenate([ranked[...], ranked[...]], axis=0).T
    wide = lax.broadcasted_iota(jnp.int32, (16, 128), 1)
    o_ref[...] = jnp.where(wide < 64, turned[0:16], turned[16:32])


def body(queries, documents, doc_lengths, candidates):
    vmem = pl.BlockSpec(memory_space=pltpu.VMEM)
    return pl.pallas_call(
        kernel,
        out_shape=jax.ShapeDtypeStruct((16, 128), jnp.float32),
        in_specs=[vmem, vmem, pl.BlockSpec(memory_space=pltpu.SMEM), vmem],
        out_specs=vmem,
        scratch_shapes=[
            pltpu.VMEM((256, 128), jnp.float32),
            pltpu.VMEM((512, 128), jnp.float32),
            pltpu.VMEM((16, 2, 128, 128), jnp.bfloat16),
            pltpu.VMEM((8, 2, 256, 128), jnp.bfloat16),
            pltpu.VMEM((16, 8, 8, 256), jnp.float32),
            pltpu.VMEM((16, 4, 128), jnp.float32),
            pltpu.VMEM((2, 16, 4, 128), jnp.float32),
            pltpu.VMEM((64, 128), jnp.float32),
            pltpu.VMEM((64, 128), jnp.float32),
            pltpu.SemaphoreType.DMA((32,)),
            pltpu.SemaphoreType.DMA((16, 2)),
            pltpu.SemaphoreType.DMA((8,)),
            pltpu.SemaphoreType.DMA((8, 2)),
            pltpu.SemaphoreType.DMA((8,)),
            pltpu.SemaphoreType.DMA((8,)),
            pltpu.SemaphoreType.DMA((16, 2)),
            pltpu.SemaphoreType.DMA((2, 16)),
        ],
        compiler_params=pltpu.CompilerParams(
            collective_id=0, has_side_effects=True, vmem_limit_bytes=32 << 20
        ),
    )(queries, documents, doc_lengths, candidates)


def solution(mesh):
    in_specs = (
        P(("query", "doc"), "tok", None),
        P(("query", "doc"), None, None),
        P(("query", "doc")),
        P(("query", "doc"), None),
    )
    out_specs = P(("query", "doc"), None)
    return jax.shard_map(body, mesh=mesh, in_specs=in_specs, out_specs=out_specs, check_vma=False)
```

```python
import jax
import jax.numpy as jnp
from jax import lax
from jax.experimental import pallas as pl
from jax.experimental.pallas import tpu as pltpu
from jax.sharding import PartitionSpec as P

MESH = pl.DeviceIdType.MESH
epsilon = 1e-06
excluded_score = -1e30

OWN, UP1, DN1, UP2, DN2, UP3, DN3, FAR = range(8)
ZOFF = (0, 7, 2, 5, 1, 6, 3, 4)


def unit_rows(values):
    widened = values.astype(jnp.float32)
    return widened * lax.rsqrt(jnp.sum(widened * widened, axis=-1, keepdims=True) + epsilon)


def kernel(
    q_hbm, d_hbm, len_hbm, cand_hbm, o_ref,
    q_ref, d_ref, len_ref, cand_ref, isem, qstage, dstage, qbuf, dbuf, peaks, outbox, inbox, live, ranked,
    qsend, qrecv, drecv, crecv, ssend, srecv,
):
    z = lax.axis_index("query")
    xy = lax.axis_index("doc")
    c = lax.axis_index("tok")
    x, y = xy // 4, xy % 4
    other = 1 - c

    def chip(dx, dy):
        return ((x + dx) % 4) * 4 + (y + dy) % 4

    near = (4, 12, 1, 3)
    axis = (8, 2)
    corner = (5, 7, 13, 15)
    far = (9, 11, 6, 14, 10)
    loads = [
        pltpu.make_async_copy(src, dst, isem.at[n])
        for n, (src, dst) in enumerate(
            ((q_hbm, q_ref), (d_hbm, d_ref), (len_hbm, len_ref), (cand_hbm, cand_ref)))
    ]
    for load in loads:
        load.start()

    barrier = pltpu.get_barrier_semaphore()

    def greet(**place):
        pl.semaphore_signal(barrier, inc=1, device_id=place, device_id_type=MESH)

    for dz in (1, 7, 2, 6):
        greet(query=(z + dz) % 8)
    for slot in near + axis + corner:
        greet(doc=chip(slot // 4, slot % 4))
    greet(tok=other)

    for load in loads:
        load.wait()

    unit = unit_rows(q_ref[...]).reshape(256, 128)
    for n in range(16):
        qstage[pl.ds(n, 16, stride=16), :] = unit[n * 16:(n + 1) * 16]
    qbuf[0] = qstage[...].astype(jnp.bfloat16).reshape(2, 128, 128)
    slots = lax.broadcasted_iota(jnp.int32, (128, 128), 0)
    for w in range(4):
        unit = unit_rows(d_ref[w])
        unit = jnp.where(slots < len_ref[w], unit, unit[0:1])
        dstage[pl.ds(w, 128, stride=4), :] = unit
    dbuf[0] = dstage[...].astype(jnp.bfloat16).reshape(2, 256, 128)

    pl.semaphore_wait(barrier, 15)

    pending = []

    def q_copy(ref_from, ref_to, recv, dx, dy):
        copy = pltpu.make_async_remote_copy(
            src_ref=ref_from, dst_ref=ref_to, send_sem=qsend.at[len(pending)], recv_sem=recv,
            device_id={"doc": chip(dx, dy)}, device_id_type=MESH,
        )
        copy.start()
        pending.append(copy)

    def q_send(slot):
        q_copy(qbuf.at[0], qbuf.at[slot], qrecv.at[slot, 0], slot // 4, slot % 4)

    def q_pass(half, slot, dx, dy):
        to = (slot // 4 + dx) % 4 * 4 + (slot % 4 + dy) % 4
        q_copy(qbuf.at[slot, half], qbuf.at[to, half], qrecv.at[to, half], dx, dy)

    def q_wait(slot, half=None):
        ref = qbuf.at[slot] if half is None else qbuf.at[slot, half]
        pltpu.make_async_remote_copy(
            src_ref=ref, dst_ref=ref, send_sem=qsend.at[0], recv_sem=qrecv.at[slot, half or 0],
            device_id={"doc": xy}, device_id_type=MESH,
        ).wait_recv()

    def z_copy(src, chunk, dz, part=None):
        rows = pl.ds(0, 256) if part is None else pl.ds(part * 128, 128)
        copy = pltpu.make_async_remote_copy(
            src_ref=dbuf.at[src, c, rows], dst_ref=dbuf.at[chunk, c, rows], send_sem=qsend.at[len(pending)],
            recv_sem=drecv.at[chunk, part or 0],
            device_id={"query": (z + dz) % 8}, device_id_type=MESH,
        )
        copy.start()
        pending.append(copy)

    def z_wait(chunk, part=None):
        rows = pl.ds(0, 256) if part is None else pl.ds(part * 128, 128)
        ref = dbuf.at[chunk, c, rows]
        pltpu.make_async_remote_copy(
            src_ref=ref, dst_ref=ref, send_sem=qsend.at[0], recv_sem=drecv.at[chunk, part or 0],
            device_id={"query": z}, device_id_type=MESH,
        ).wait_recv()

    def share(chunk):
        copy = pltpu.make_async_remote_copy(
            src_ref=dbuf.at[chunk, c], dst_ref=dbuf.at[chunk, c], send_sem=qsend.at[len(pending)],
            recv_sem=crecv.at[chunk], device_id={"tok": other}, device_id_type=MESH,
        )
        copy.start()
        pending.append(copy)

    def share_wait(chunk):
        ref = dbuf.at[chunk, other]
        pltpu.make_async_remote_copy(
            src_ref=ref, dst_ref=ref, send_sem=qsend.at[0], recv_sem=crecv.at[chunk],
            device_id={"tok": c}, device_id_type=MESH,
        ).wait_recv()

    def match(slot, chunks):
        tokens = qbuf[slot].reshape(256, 128)
        for k in chunks:
            similar = lax.dot_general(
                dbuf[k].reshape(512, 128), tokens, (((1,), (1,)), ((), ())),
                preferred_element_type=jnp.float32,
            )
            peaks[slot, k] = jnp.max(similar.reshape(64, 8, 256), axis=0)

    sub = lax.broadcasted_iota(jnp.int32, (8, 128), 0)
    lane = lax.broadcasted_iota(jnp.int32, (8, 128), 1)

    def total(slot):
        pairs = []
        for p in range(4):
            both = 0.0
            for h in range(2):
                a = peaks[slot, 2 * p, :, h * 128:(h + 1) * 128]
                b = peaks[slot, 2 * p + 1, :, h * 128:(h + 1) * 128]
                first = jnp.where(sub < 4, a, b)
                second = jnp.where(sub < 4, b, a)
                both = both + jnp.maximum(first, pltpu.roll(second, 4, 0))
            pairs.append(both)
        low = lane < 64
        folded = []
        for p in (0, 2):
            a, b = pairs[p], pairs[p + 1]
            folded.append(jnp.where(low, a, b) + pltpu.roll(jnp.where(low, b, a), 64, 1))
        f0, f1 = folded
        quarter = jnp.where((lane & 63) < 32, f0 + pltpu.roll(f0, 96, 1), f1 + pltpu.roll(f1, 32, 1))
        even = quarter + pltpu.roll(quarter, 112, 1)
        odd = quarter + pltpu.roll(quarter, 16, 1)
        return jnp.where((lane & 31) < 16, even, pltpu.roll(odd, 4, 0))[0:4]

    def score_copy(slot, tok):
        return pltpu.make_async_remote_copy(
            src_ref=outbox.at[slot], dst_ref=inbox.at[c, slot], send_sem=ssend.at[slot, tok],
            recv_sem=srecv.at[c, slot],
            device_id={"doc": ((x - slot // 4 + 4) % 4) * 4 + (y - slot % 4 + 4) % 4, "tok": tok},
            device_id_type=MESH,
        )

    z_copy(OWN, UP1, 1)
    z_copy(OWN, DN1, 7)
    for slot in near:
        q_send(slot)
    z_copy(OWN, UP2, 2)
    z_copy(OWN, DN2, 6)
    for slot in axis:
        q_send(slot)
    for slot in corner:
        q_send(slot)

    rows = lax.broadcasted_iota(jnp.int32, (64, 256), 0)
    source = rows >> 2
    row_id = (((x + (source >> 2)) & 3) * 4 + ((y + source) & 3)) * 4 + (rows & 3)
    lanes = lax.broadcasted_iota(jnp.int32, (128, 256), 0)
    group = lanes >> 4
    plane = jnp.zeros_like(group)
    for g in range(8):
        plane = jnp.where(group == g, (z + ZOFF[g]) % 8, plane)
    first = cand_ref[0:1, :]
    second = cand_ref[1:2, :]
    listed = jnp.where((lanes & 15) < 8, first, second)
    by_plane = jnp.where(listed >> 6 == plane, 1.0, 0.0).astype(jnp.bfloat16)
    found = []
    for block in (first, second):
        by_row = jnp.where(block & 63 == row_id, 1.0, 0.0).astype(jnp.bfloat16)
        found.append(lax.dot_general(
            by_row, by_plane, (((1,), (1,)), ((), ())), preferred_element_type=jnp.float32))
    wide_lane = lax.broadcasted_iota(jnp.int32, (64, 128), 1)
    live[...] = jnp.where((wide_lane & 15) < 8, found[0], found[1])

    match(0, (OWN,))

    for s in near:
        q_wait(s)
    q_pass(1, 1, 2, 0)
    q_pass(1, 3, 2, 0)
    q_pass(0, 4, 0, 2)
    q_pass(0, 12, 0, 2)
    z_wait(UP1)
    share(UP1)
    z_copy(UP1, UP3, 2)
    z_wait(DN1)
    share(DN1)
    z_copy(DN1, DN3, 6)
    for s in near:
        match(s, (OWN,))
    share_wait(UP1)
    share_wait(DN1)
    for s in (0,) + near:
        match(s, (UP1, DN1))

    q_wait(8)
    q_wait(2)
    for d in (1, 3, 2):
        q_pass(0, 8, 0, d)
        q_pass(1, 2, d, 0)
    z_wait(UP2)
    z_copy(UP2, FAR, 2, 0)
    share(UP2)
    z_wait(DN2)
    z_copy(DN2, FAR, 6, 1)
    share(DN2)
    for s in axis:
        match(s, (OWN, UP1, DN1))
    share_wait(UP2)
    share_wait(DN2)
    for s in (0,) + near + axis:
        match(s, (UP2, DN2))

    for s in corner:
        q_wait(s)
    for s in corner:
        match(s, (OWN, UP1, DN1, UP2, DN2))

    z_wait(UP3)
    share(UP3)
    z_wait(DN3)
    share(DN3)
    for s in far:
        q_wait(s, 0)
        q_wait(s, 1)
    for s in far:
        match(s, (OWN, UP1, DN1, UP2, DN2))
    z_wait(FAR, 0)
    z_wait(FAR, 1)
    share(FAR)
    share_wait(UP3)
    share_wait(DN3)
    for s in far + corner + axis + near + (0,):
        match(s, (UP3, DN3))
    share_wait(FAR)

    def deliver(slots):
        for s in slots:
            if s:
                score_copy(s, 0).start()
                score_copy(s, 1).start()

    waves = (far, corner, axis + near[:2], near[2:] + (0,))
    for n, wave in enumerate(waves):
        for s in wave:
            match(s, (FAR,))
        if n:
            for s in waves[n - 1]:
                outbox[s] = total(s)
            deliver(waves[n - 1])
    sums = [total(s) for s in waves[-1]]
    for s, value in zip(waves[-1], sums):
        outbox[s] = value
    inbox[c, 0] = sums[-1]
    deliver(waves[-1])
    sibling = pltpu.make_async_remote_copy(
        src_ref=outbox.at[0], dst_ref=inbox.at[c, 0], send_sem=ssend.at[0, 0], recv_sem=srecv.at[c, 0],
        device_id={"tok": other}, device_id_type=MESH,
    )
    sibling.start()

    def arrive(tok, slot):
        ref = inbox.at[tok, slot]
        pltpu.make_async_remote_copy(
            src_ref=ref, dst_ref=ref, send_sem=ssend.at[0, 0], recv_sem=srecv.at[tok, slot],
            device_id={"tok": other}, device_id_type=MESH,
        ).wait_recv()

    arrive(other, 0)
    for slot in range(1, 16):
        arrive(0, slot)
        arrive(1, slot)

    regs = []
    for v in range(8):
        pieces = [inbox[0, 2 * v + h] + inbox[1, 2 * v + h] for h in (0, 1)]
        value = jnp.concatenate(pieces, axis=0)
        regs.append(jnp.where(live[v * 8:(v + 1) * 8] > 0.0, value, excluded_score))

    def bit(k):
        return (sub >> (k - 3)) & 1 if k < 6 else (lane >> (k - 2)) & 1

    def partner(value, k):
        if k < 6:
            axis, step, size = 0, 1 << (k - 3), 8
        else:
            axis, step, size = 1, 1 << (k - 2), 128
        if 2 * step == size:
            return pltpu.roll(value, step, axis)
        return jnp.where(bit(k) == 0, pltpu.roll(value, size - step, axis), pltpu.roll(value, step, axis))

    def exchange(regs, k, flips=None):
        if k < 3:
            out = list(regs)
            for v in range(8):
                if v & (1 << k):
                    continue
                u = v | (1 << k)
                high, low = jnp.maximum(regs[v], regs[u]), jnp.minimum(regs[v], regs[u])
                if flips is not None and v & (1 << flips):
                    high, low = low, high
                out[v], out[u] = high, low
            return out
        keep_high = bit(k) == 0
        out = []
        for r in regs:
            mate = partner(r, k)
            out.append(jnp.where(keep_high, jnp.maximum(r, mate), jnp.minimum(r, mate)))
        return out

    def signed(regs, k):
        return [jnp.where(bit(k) == 0, r, -r) for r in regs]

    for phase in range(1, 10):
        top = min(phase - 1, 6)
        if phase in (8, 9):
            regs = [jnp.maximum(r, partner(r, phase - 1)) for r in regs]
        by_mask = 3 <= phase < 9
        if by_mask:
            regs = signed(regs, phase)
        for k in range(top, -1, -1):
            regs = exchange(regs, k, phase if phase < 3 else None)
        if by_mask:
            regs = signed(regs, phase)

    for v in range(8):
        ranked[pl.ds(v, 8, stride=8), :] = regs[v]
    turned = jnp.concatenate([ranked[...], ranked[...]], axis=0).T
    wide = lax.broadcasted_iota(jnp.int32, (16, 128), 1)
    o_ref[...] = jnp.where(wide < 64, turned[0:16], turned[16:32])

    for copy in pending:
        copy.wait_send()
    for slot in range(1, 16):
        score_copy(slot, 0).wait_send()
        score_copy(slot, 1).wait_send()
    sibling.wait_send()


def body(queries, documents, doc_lengths, candidates):
    vmem = pl.BlockSpec(memory_space=pltpu.VMEM)
    return pl.pallas_call(
        kernel,
        out_shape=jax.ShapeDtypeStruct((16, 128), jnp.float32),
        in_specs=[pl.BlockSpec(memory_space=pltpu.HBM)] * 4,
        out_specs=vmem,
        scratch_shapes=[
            pltpu.VMEM((16, 16, 128), jnp.bfloat16),
            pltpu.VMEM((4, 128, 128), jnp.bfloat16),
            pltpu.SMEM((4,), jnp.int32),
            pltpu.VMEM((2, 256), jnp.int32),
            pltpu.SemaphoreType.DMA((4,)),
            pltpu.VMEM((256, 128), jnp.float32),
            pltpu.VMEM((512, 128), jnp.float32),
            pltpu.VMEM((16, 2, 128, 128), jnp.bfloat16),
            pltpu.VMEM((8, 2, 256, 128), jnp.bfloat16),
            pltpu.VMEM((16, 8, 8, 256), jnp.float32),
            pltpu.VMEM((16, 4, 128), jnp.float32),
            pltpu.VMEM((2, 16, 4, 128), jnp.float32),
            pltpu.VMEM((64, 128), jnp.float32),
            pltpu.VMEM((64, 128), jnp.float32),
            pltpu.SemaphoreType.DMA((40,)),
            pltpu.SemaphoreType.DMA((16, 2)),
            pltpu.SemaphoreType.DMA((8, 2)),
            pltpu.SemaphoreType.DMA((8,)),
            pltpu.SemaphoreType.DMA((16, 2)),
            pltpu.SemaphoreType.DMA((2, 16)),
        ],
        compiler_params=pltpu.CompilerParams(
            collective_id=0, has_side_effects=True, vmem_limit_bytes=60 << 20
        ),
    )(queries, documents, doc_lengths, candidates)


def solution(mesh):
    in_specs = (
        P(("query", "doc"), "tok", None),
        P(("query", "doc"), None, None),
        P(("query", "doc")),
        P(("query", "doc"), None),
    )
    out_specs = P(("query", "doc"), None)
    return jax.shard_map(body, mesh=mesh, in_specs=in_specs, out_specs=out_specs, check_vma=False)
```

```python
import jax
import jax.numpy as jnp
from jax import lax
from jax.experimental import pallas as pl
from jax.experimental.pallas import tpu as pltpu
from jax.sharding import PartitionSpec as P

MESH = pl.DeviceIdType.MESH
epsilon = 1e-06
excluded_score = -1e30

OWN, UP1, DN1, UP2, DN2, UP3, DN3, FAR = range(8)
ZOFF = (0, 7, 2, 5, 1, 6, 3, 4)


def unit_rows(values):
    widened = values.astype(jnp.float32)
    return widened * lax.rsqrt(jnp.sum(widened * widened, axis=-1, keepdims=True) + epsilon)


def kernel(
    q_hbm, d_hbm, len_hbm, cand_hbm, o_ref,
    q_ref, d_ref, len_ref, cand_ref, isem, qstage, dstage, qbuf, dbuf, peaks, outbox, inbox, live, ranked,
    qsend, qrecv, drecv, crecv, ssend, srecv,
):
    z = lax.axis_index("query")
    xy = lax.axis_index("doc")
    c = lax.axis_index("tok")
    x, y = xy // 4, xy % 4
    other = 1 - c

    def chip(dx, dy):
        return ((x + dx) % 4) * 4 + (y + dy) % 4

    near = (4, 12, 1, 3)
    axis = (8, 2)
    corner = (5, 7, 13, 15)
    far = (9, 11, 6, 14, 10)
    loads = [
        pltpu.make_async_copy(src, dst, isem.at[n])
        for n, (src, dst) in enumerate(
            ((q_hbm, q_ref), (d_hbm, d_ref), (len_hbm, len_ref), (cand_hbm, cand_ref)))
    ]
    for load in loads:
        load.start()

    barrier = pltpu.get_barrier_semaphore()

    def greet(**place):
        pl.semaphore_signal(barrier, inc=1, device_id=place, device_id_type=MESH)

    for dz in (1, 7, 2, 6):
        greet(query=(z + dz) % 8)
    for slot in near + axis:
        greet(doc=chip(slot // 4, slot % 4))
    greet(tok=other)

    for load in loads:
        load.wait()

    unit = unit_rows(q_ref[...]).reshape(256, 128)
    for n in range(16):
        qstage[pl.ds(n, 16, stride=16), :] = unit[n * 16:(n + 1) * 16]
    qbuf[0] = qstage[...].astype(jnp.bfloat16).reshape(2, 128, 128)
    slots = lax.broadcasted_iota(jnp.int32, (128, 128), 0)
    for w in range(4):
        unit = unit_rows(d_ref[w])
        unit = jnp.where(slots < len_ref[w], unit, unit[0:1])
        dstage[pl.ds(w, 128, stride=4), :] = unit
    dbuf[:, OWN] = dstage[...].astype(jnp.bfloat16).reshape(2, 256, 128)

    pl.semaphore_wait(barrier, 11)

    pending = []

    def q_copy(ref_from, ref_to, recv, dx, dy):
        copy = pltpu.make_async_remote_copy(
            src_ref=ref_from, dst_ref=ref_to, send_sem=qsend.at[len(pending)], recv_sem=recv,
            device_id={"doc": chip(dx, dy)}, device_id_type=MESH,
        )
        copy.start()
        pending.append(copy)

    def q_send(slot):
        q_copy(qbuf.at[0], qbuf.at[slot], qrecv.at[slot, 0], slot // 4, slot % 4)

    def q_pass(half, slot, dx, dy):
        to = (slot // 4 + dx) % 4 * 4 + (slot % 4 + dy) % 4
        q_copy(qbuf.at[slot, half], qbuf.at[to, half], qrecv.at[to, half], dx, dy)

    def q_wait(slot, half=None):
        ref = qbuf.at[slot] if half is None else qbuf.at[slot, half]
        pltpu.make_async_remote_copy(
            src_ref=ref, dst_ref=ref, send_sem=qsend.at[0], recv_sem=qrecv.at[slot, half or 0],
            device_id={"doc": xy}, device_id_type=MESH,
        ).wait_recv()

    def z_copy(src, chunk, dz, part=None):
        rows = pl.ds(0, 256) if part is None else pl.ds(part * 128, 128)
        copy = pltpu.make_async_remote_copy(
            src_ref=dbuf.at[c, src, rows], dst_ref=dbuf.at[c, chunk, rows], send_sem=qsend.at[len(pending)],
            recv_sem=drecv.at[chunk, part or 0],
            device_id={"query": (z + dz) % 8}, device_id_type=MESH,
        )
        copy.start()
        pending.append(copy)

    def z_wait(chunk, part=None):
        rows = pl.ds(0, 256) if part is None else pl.ds(part * 128, 128)
        ref = dbuf.at[c, chunk, rows]
        pltpu.make_async_remote_copy(
            src_ref=ref, dst_ref=ref, send_sem=qsend.at[0], recv_sem=drecv.at[chunk, part or 0],
            device_id={"query": z}, device_id_type=MESH,
        ).wait_recv()

    def share(chunk):
        copy = pltpu.make_async_remote_copy(
            src_ref=dbuf.at[c, chunk], dst_ref=dbuf.at[c, chunk], send_sem=qsend.at[len(pending)],
            recv_sem=crecv.at[chunk], device_id={"tok": other}, device_id_type=MESH,
        )
        copy.start()
        pending.append(copy)

    def share_wait(chunk):
        ref = dbuf.at[other, chunk]
        pltpu.make_async_remote_copy(
            src_ref=ref, dst_ref=ref, send_sem=qsend.at[0], recv_sem=crecv.at[chunk],
            device_id={"tok": c}, device_id_type=MESH,
        ).wait_recv()

    def match(slots, start, count, halves):
        for half in halves:
            joins = half is other
            for slot in slots:
                similar = lax.dot_general(
                    dbuf[half, start:start + count].reshape(count * 256, 128), qbuf[slot].reshape(256, 128),
                    (((1,), (1,)), ((), ())), preferred_element_type=jnp.float32,
                )
                best = jnp.max(similar.reshape(count, 32, 8, 256), axis=1)
                if joins:
                    best = jnp.maximum(best, peaks[slot, start:start + count])
                peaks[slot, start:start + count] = best

    sub = lax.broadcasted_iota(jnp.int32, (8, 128), 0)
    lane = lax.broadcasted_iota(jnp.int32, (8, 128), 1)

    def total(slot):
        pairs = []
        for p in range(4):
            both = 0.0
            for h in range(2):
                a = peaks[slot, 2 * p, :, h * 128:(h + 1) * 128]
                b = peaks[slot, 2 * p + 1, :, h * 128:(h + 1) * 128]
                first = jnp.where(sub < 4, a, b)
                second = jnp.where(sub < 4, b, a)
                both = both + jnp.maximum(first, pltpu.roll(second, 4, 0))
            pairs.append(both)
        low = lane < 64
        folded = []
        for p in (0, 2):
            a, b = pairs[p], pairs[p + 1]
            folded.append(jnp.where(low, a, b) + pltpu.roll(jnp.where(low, b, a), 64, 1))
        f0, f1 = folded
        quarter = jnp.where((lane & 63) < 32, f0 + pltpu.roll(f0, 96, 1), f1 + pltpu.roll(f1, 32, 1))
        even = quarter + pltpu.roll(quarter, 112, 1)
        odd = quarter + pltpu.roll(quarter, 16, 1)
        return jnp.where((lane & 31) < 16, even, pltpu.roll(odd, 4, 0))[0:4]

    def score_copy(slot, tok):
        return pltpu.make_async_remote_copy(
            src_ref=outbox.at[slot], dst_ref=inbox.at[c, slot], send_sem=ssend.at[slot, tok],
            recv_sem=srecv.at[c, slot],
            device_id={"doc": ((x - slot // 4 + 4) % 4) * 4 + (y - slot % 4 + 4) % 4, "tok": tok},
            device_id_type=MESH,
        )

    z_copy(OWN, UP2, 2, 0)
    z_copy(OWN, DN2, 6, 1)
    for slot in near[:2]:
        q_send(slot)
    z_copy(OWN, UP1, 1)
    z_copy(OWN, DN1, 7)
    for slot in near[2:]:
        q_send(slot)
    for slot in axis:
        q_send(slot)
    z_copy(OWN, UP2, 2, 1)
    z_copy(OWN, DN2, 6, 0)

    rows = lax.broadcasted_iota(jnp.int32, (64, 256), 0)
    source = rows >> 2
    row_id = (((x + (source >> 2)) & 3) * 4 + ((y + source) & 3)) * 4 + (rows & 3)
    lanes = lax.broadcasted_iota(jnp.int32, (128, 256), 0)
    group = lanes >> 4
    plane = jnp.zeros_like(group)
    for g in range(8):
        plane = jnp.where(group == g, (z + ZOFF[g]) % 8, plane)
    first = cand_ref[0:1, :]
    second = cand_ref[1:2, :]
    listed = jnp.where((lanes & 15) < 8, first, second)
    by_plane = jnp.where(listed >> 6 == plane, 1.0, 0.0).astype(jnp.bfloat16)
    found = []
    for block in (first, second):
        by_row = jnp.where(block & 63 == row_id, 1.0, 0.0).astype(jnp.bfloat16)
        found.append(lax.dot_general(
            by_row, by_plane, (((1,), (1,)), ((), ())), preferred_element_type=jnp.float32))
    wide_lane = lax.broadcasted_iota(jnp.int32, (64, 128), 1)
    live[...] = jnp.where((wide_lane & 15) < 8, found[0], found[1])

    both = (c, other)
    match((0,), OWN, 1, both)

    q_wait(4)
    q_pass(0, 4, 0, 1)
    q_pass(0, 4, 0, 3)
    q_wait(12)
    q_pass(0, 12, 0, 1)
    q_pass(0, 12, 0, 3)
    q_wait(1)
    q_pass(1, 1, 1, 0)
    q_pass(1, 1, 3, 0)
    q_wait(3)
    q_pass(1, 3, 1, 0)
    q_pass(1, 3, 3, 0)
    z_wait(UP2, 0)
    z_copy(UP2, FAR, 2, 0)
    z_copy(UP2, UP3, 1, 0)
    z_wait(DN2, 1)
    z_copy(DN2, FAR, 6, 1)
    z_copy(DN2, DN3, 7, 1)
    z_wait(UP1)
    share(UP1)
    z_wait(DN1)
    share(DN1)
    q_pass(0, 4, 0, 2)
    q_pass(0, 12, 0, 2)
    q_pass(1, 1, 2, 0)
    q_pass(1, 3, 2, 0)
    match(near, OWN, 1, both)
    q_wait(8)
    q_wait(2)
    for d in (1, 3, 2):
        q_pass(0, 8, 0, d)
        q_pass(1, 2, d, 0)
    inner = (0,) + near + axis
    match(inner, UP1, 2, (c,))
    z_wait(UP2, 1)
    z_copy(UP2, UP3, 1, 1)
    share(UP2)
    z_wait(DN2, 0)
    z_copy(DN2, DN3, 7, 0)
    share(DN2)
    match(axis, OWN, 1, both)
    share_wait(UP1)
    share_wait(DN1)
    match(inner, UP1, 2, (other,))
    match(inner, UP2, 2, (c,))
    share_wait(UP2)
    share_wait(DN2)
    match(inner, UP2, 2, (other,))

    for s in corner:
        q_wait(s, 0)
        q_wait(s, 1)
        match((s,), OWN, 5, both)
    for part in (0, 1):
        z_wait(UP3, part)
    share(UP3)
    for part in (1, 0):
        z_wait(DN3, part)
    share(DN3)
    for s in far[:2]:
        q_wait(s, 0)
        q_wait(s, 1)
        match((s,), OWN, 5, both)
    z_wait(FAR, 0)
    z_wait(FAR, 1)
    share(FAR)
    for s in far[2:]:
        q_wait(s, 0)
        q_wait(s, 1)
        match((s,), OWN, 5, both)
    match(range(16), UP3, 3, (c,))
    share_wait(UP3)
    share_wait(DN3)
    share_wait(FAR)

    def deliver(slots):
        for s in slots:
            if s:
                score_copy(s, 0).start()
                score_copy(s, 1).start()

    waves = (far, corner, axis + near[:2], near[2:] + (0,))
    for n, wave in enumerate(waves):
        match(wave, UP3, 3, (other,))
        if n:
            for s in waves[n - 1]:
                outbox[s] = total(s)
            deliver(waves[n - 1])
    sums = [total(s) for s in waves[-1]]
    for s, value in zip(waves[-1], sums):
        outbox[s] = value
    inbox[c, 0] = sums[-1]
    deliver(waves[-1])
    sibling = pltpu.make_async_remote_copy(
        src_ref=outbox.at[0], dst_ref=inbox.at[c, 0], send_sem=ssend.at[0, 0], recv_sem=srecv.at[c, 0],
        device_id={"tok": other}, device_id_type=MESH,
    )
    sibling.start()

    def arrive(tok, slot):
        ref = inbox.at[tok, slot]
        pltpu.make_async_remote_copy(
            src_ref=ref, dst_ref=ref, send_sem=ssend.at[0, 0], recv_sem=srecv.at[tok, slot],
            device_id={"tok": other}, device_id_type=MESH,
        ).wait_recv()

    arrive(other, 0)
    for slot in range(1, 16):
        arrive(0, slot)
        arrive(1, slot)

    regs = []
    for v in range(8):
        pieces = [inbox[0, 2 * v + h] + inbox[1, 2 * v + h] for h in (0, 1)]
        value = jnp.concatenate(pieces, axis=0)
        regs.append(jnp.where(live[v * 8:(v + 1) * 8] > 0.0, value, excluded_score))

    def bit(k):
        return (sub >> (k - 3)) & 1 if k < 6 else (lane >> (k - 2)) & 1

    def partner(value, k):
        if k < 6:
            axis, step, size = 0, 1 << (k - 3), 8
        else:
            axis, step, size = 1, 1 << (k - 2), 128
        if 2 * step == size:
            return pltpu.roll(value, step, axis)
        return jnp.where(bit(k) == 0, pltpu.roll(value, size - step, axis), pltpu.roll(value, step, axis))

    def exchange(regs, k, flips=None):
        if k < 3:
            out = list(regs)
            for v in range(8):
                if v & (1 << k):
                    continue
                u = v | (1 << k)
                high, low = jnp.maximum(regs[v], regs[u]), jnp.minimum(regs[v], regs[u])
                if flips is not None and v & (1 << flips):
                    high, low = low, high
                out[v], out[u] = high, low
            return out
        keep_high = bit(k) == 0
        out = []
        for r in regs:
            mate = partner(r, k)
            out.append(jnp.where(keep_high, jnp.maximum(r, mate), jnp.minimum(r, mate)))
        return out

    def signed(regs, k):
        return [jnp.where(bit(k) == 0, r, -r) for r in regs]

    for phase in range(1, 10):
        top = min(phase - 1, 6)
        if phase in (8, 9):
            regs = [jnp.maximum(r, partner(r, phase - 1)) for r in regs]
        by_mask = 3 <= phase < 9
        if by_mask:
            regs = signed(regs, phase)
        for k in range(top, -1, -1):
            regs = exchange(regs, k, phase if phase < 3 else None)
        if by_mask:
            regs = signed(regs, phase)

    for v in range(8):
        ranked[pl.ds(v, 8, stride=8), :] = regs[v]
    turned = jnp.concatenate([ranked[...], ranked[...]], axis=0).T
    wide = lax.broadcasted_iota(jnp.int32, (16, 128), 1)
    o_ref[...] = jnp.where(wide < 64, turned[0:16], turned[16:32])

    for copy in pending:
        copy.wait_send()
    for slot in range(1, 16):
        score_copy(slot, 0).wait_send()
        score_copy(slot, 1).wait_send()
    sibling.wait_send()


def body(queries, documents, doc_lengths, candidates):
    vmem = pl.BlockSpec(memory_space=pltpu.VMEM)
    return pl.pallas_call(
        kernel,
        out_shape=jax.ShapeDtypeStruct((16, 128), jnp.float32),
        in_specs=[pl.BlockSpec(memory_space=pltpu.HBM)] * 4,
        out_specs=vmem,
        scratch_shapes=[
            pltpu.VMEM((16, 16, 128), jnp.bfloat16),
            pltpu.VMEM((4, 128, 128), jnp.bfloat16),
            pltpu.SMEM((4,), jnp.int32),
            pltpu.VMEM((2, 256), jnp.int32),
            pltpu.SemaphoreType.DMA((4,)),
            pltpu.VMEM((256, 128), jnp.float32),
            pltpu.VMEM((512, 128), jnp.float32),
            pltpu.VMEM((16, 2, 128, 128), jnp.bfloat16),
            pltpu.VMEM((2, 8, 256, 128), jnp.bfloat16),
            pltpu.VMEM((16, 8, 8, 256), jnp.float32),
            pltpu.VMEM((16, 4, 128), jnp.float32),
            pltpu.VMEM((2, 16, 4, 128), jnp.float32),
            pltpu.VMEM((64, 128), jnp.float32),
            pltpu.VMEM((64, 128), jnp.float32),
            pltpu.SemaphoreType.DMA((48,)),
            pltpu.SemaphoreType.DMA((16, 2)),
            pltpu.SemaphoreType.DMA((8, 2)),
            pltpu.SemaphoreType.DMA((8,)),
            pltpu.SemaphoreType.DMA((16, 2)),
            pltpu.SemaphoreType.DMA((2, 16)),
        ],
        compiler_params=pltpu.CompilerParams(
            collective_id=0, has_side_effects=True, vmem_limit_bytes=60 << 20
        ),
    )(queries, documents, doc_lengths, candidates)


def solution(mesh):
    in_specs = (
        P(("query", "doc"), "tok", None),
        P(("query", "doc"), None, None),
        P(("query", "doc")),
        P(("query", "doc"), None),
    )
    out_specs = P(("query", "doc"), None)
    return jax.shard_map(body, mesh=mesh, in_specs=in_specs, out_specs=out_specs, check_vma=False)
```

```python
import jax
import jax.numpy as jnp
from jax import lax
from jax.experimental import pallas as pl
from jax.experimental.pallas import tpu as pltpu
from jax.sharding import PartitionSpec as P

MESH = pl.DeviceIdType.MESH
epsilon = 1e-06
excluded_score = -1e30

OWN, UP1, DN1, UP2, DN2, UP3, DN3, FAR = range(8)
ZOFF = (0, 7, 2, 5, 1, 6, 3, 4)


def unit_rows(values):
    widened = values.astype(jnp.float32)
    return widened * lax.rsqrt(jnp.sum(widened * widened, axis=-1, keepdims=True) + epsilon)


def kernel(
    q_hbm, d_hbm, len_hbm, cand_hbm, o_ref,
    q_ref, d_ref, len_ref, cand_ref, isem, qstage, dstage, qbuf, dbuf, peaks, outbox, inbox, live, ranked,
    qsend, qrecv, drecv, crecv, ssend, srecv,
):
    z = lax.axis_index("query")
    xy = lax.axis_index("doc")
    c = lax.axis_index("tok")
    x, y = xy // 4, xy % 4
    other = 1 - c

    def chip(dx, dy):
        return ((x + dx) % 4) * 4 + (y + dy) % 4

    near = (4, 12, 1, 3)
    axis = (8, 2)
    corner = (5, 7, 13, 15)
    far = (9, 11, 6, 14, 10)
    loads = [
        pltpu.make_async_copy(src, dst, isem.at[n])
        for n, (src, dst) in enumerate(
            ((d_hbm, d_ref), (len_hbm, len_ref), (q_hbm, q_ref), (cand_hbm, cand_ref)))
    ]
    for load in loads:
        load.start()

    barrier = pltpu.get_barrier_semaphore()

    def greet(**place):
        pl.semaphore_signal(barrier, inc=1, device_id=place, device_id_type=MESH)

    for dz in (1, 7, 2, 6):
        greet(query=(z + dz) % 8)
    for slot in near + axis:
        greet(doc=chip(slot // 4, slot % 4))
    greet(tok=other)

    loads[0].wait()
    loads[1].wait()
    slots = lax.broadcasted_iota(jnp.int32, (128, 128), 0)
    for w in range(4):
        unit = unit_rows(d_ref[w])
        unit = jnp.where(slots < len_ref[w], unit, unit[0:1])
        dstage[pl.ds(w, 128, stride=4), :] = unit
    dbuf[:, OWN] = dstage[...].astype(jnp.bfloat16).reshape(2, 256, 128)

    pl.semaphore_wait(barrier, 11)

    pending = []

    def q_copy(ref_from, ref_to, recv, dx, dy):
        copy = pltpu.make_async_remote_copy(
            src_ref=ref_from, dst_ref=ref_to, send_sem=qsend.at[len(pending)], recv_sem=recv,
            device_id={"doc": chip(dx, dy)}, device_id_type=MESH,
        )
        copy.start()
        pending.append(copy)

    def q_send(slot):
        q_copy(qbuf.at[0], qbuf.at[slot], qrecv.at[slot, 0], slot // 4, slot % 4)

    def q_pass(half, slot, dx, dy):
        to = (slot // 4 + dx) % 4 * 4 + (slot % 4 + dy) % 4
        q_copy(qbuf.at[slot, half], qbuf.at[to, half], qrecv.at[to, half], dx, dy)

    def q_wait(slot, half=None):
        ref = qbuf.at[slot] if half is None else qbuf.at[slot, half]
        pltpu.make_async_remote_copy(
            src_ref=ref, dst_ref=ref, send_sem=qsend.at[0], recv_sem=qrecv.at[slot, half or 0],
            device_id={"doc": xy}, device_id_type=MESH,
        ).wait_recv()

    def z_copy(src, chunk, dz, part=None):
        rows = pl.ds(0, 256) if part is None else pl.ds(part * 128, 128)
        copy = pltpu.make_async_remote_copy(
            src_ref=dbuf.at[c, src, rows], dst_ref=dbuf.at[c, chunk, rows], send_sem=qsend.at[len(pending)],
            recv_sem=drecv.at[chunk, part or 0],
            device_id={"query": (z + dz) % 8}, device_id_type=MESH,
        )
        copy.start()
        pending.append(copy)

    def z_wait(chunk, part=None):
        rows = pl.ds(0, 256) if part is None else pl.ds(part * 128, 128)
        ref = dbuf.at[c, chunk, rows]
        pltpu.make_async_remote_copy(
            src_ref=ref, dst_ref=ref, send_sem=qsend.at[0], recv_sem=drecv.at[chunk, part or 0],
            device_id={"query": z}, device_id_type=MESH,
        ).wait_recv()

    def share(chunk):
        copy = pltpu.make_async_remote_copy(
            src_ref=dbuf.at[c, chunk], dst_ref=dbuf.at[c, chunk], send_sem=qsend.at[len(pending)],
            recv_sem=crecv.at[chunk], device_id={"tok": other}, device_id_type=MESH,
        )
        copy.start()
        pending.append(copy)

    def share_wait(chunk):
        ref = dbuf.at[other, chunk]
        pltpu.make_async_remote_copy(
            src_ref=ref, dst_ref=ref, send_sem=qsend.at[0], recv_sem=crecv.at[chunk],
            device_id={"tok": c}, device_id_type=MESH,
        ).wait_recv()

    def match(slots, start, count, halves):
        for half in halves:
            joins = half is other
            for slot in slots:
                similar = lax.dot_general(
                    dbuf[half, start:start + count].reshape(count * 256, 128), qbuf[slot].reshape(256, 128),
                    (((1,), (1,)), ((), ())), preferred_element_type=jnp.float32,
                )
                best = jnp.max(similar.reshape(count, 32, 8, 256), axis=1)
                if joins:
                    best = jnp.maximum(best, peaks[slot, start:start + count])
                peaks[slot, start:start + count] = best

    sub = lax.broadcasted_iota(jnp.int32, (8, 128), 0)
    lane = lax.broadcasted_iota(jnp.int32, (8, 128), 1)

    def total(slot):
        pairs = []
        for p in range(4):
            both = 0.0
            for h in range(2):
                a = peaks[slot, 2 * p, :, h * 128:(h + 1) * 128]
                b = peaks[slot, 2 * p + 1, :, h * 128:(h + 1) * 128]
                first = jnp.where(sub < 4, a, b)
                second = jnp.where(sub < 4, b, a)
                both = both + jnp.maximum(first, pltpu.roll(second, 4, 0))
            pairs.append(both)
        low = lane < 64
        folded = []
        for p in (0, 2):
            a, b = pairs[p], pairs[p + 1]
            folded.append(jnp.where(low, a, b) + pltpu.roll(jnp.where(low, b, a), 64, 1))
        f0, f1 = folded
        quarter = jnp.where((lane & 63) < 32, f0 + pltpu.roll(f0, 96, 1), f1 + pltpu.roll(f1, 32, 1))
        even = quarter + pltpu.roll(quarter, 112, 1)
        odd = quarter + pltpu.roll(quarter, 16, 1)
        return jnp.where((lane & 31) < 16, even, pltpu.roll(odd, 4, 0))[0:4]

    def score_copy(slot, tok):
        return pltpu.make_async_remote_copy(
            src_ref=outbox.at[slot], dst_ref=inbox.at[c, slot], send_sem=ssend.at[slot, tok],
            recv_sem=srecv.at[c, slot],
            device_id={"doc": ((x - slot // 4 + 4) % 4) * 4 + (y - slot % 4 + 4) % 4, "tok": tok},
            device_id_type=MESH,
        )

    z_copy(OWN, UP2, 2, 0)
    z_copy(OWN, DN2, 6, 1)
    z_copy(OWN, UP1, 1)
    z_copy(OWN, DN1, 7)

    loads[2].wait()
    unit = unit_rows(q_ref[...]).reshape(256, 128)
    for n in range(16):
        qstage[pl.ds(n, 16, stride=16), :] = unit[n * 16:(n + 1) * 16]
    qbuf[0] = qstage[...].astype(jnp.bfloat16).reshape(2, 128, 128)
    for slot in near + axis:
        q_send(slot)
    z_copy(OWN, UP2, 2, 1)
    z_copy(OWN, DN2, 6, 0)
    loads[3].wait()

    rows = lax.broadcasted_iota(jnp.int32, (64, 256), 0)
    source = rows >> 2
    row_id = (((x + (source >> 2)) & 3) * 4 + ((y + source) & 3)) * 4 + (rows & 3)
    lanes = lax.broadcasted_iota(jnp.int32, (128, 256), 0)
    group = lanes >> 4
    plane = jnp.zeros_like(group)
    for g in range(8):
        plane = jnp.where(group == g, (z + ZOFF[g]) % 8, plane)
    first = cand_ref[0:1, :]
    second = cand_ref[1:2, :]
    listed = jnp.where((lanes & 15) < 8, first, second)
    by_plane = jnp.where(listed >> 6 == plane, 1.0, 0.0).astype(jnp.bfloat16)
    found = []
    for block in (first, second):
        by_row = jnp.where(block & 63 == row_id, 1.0, 0.0).astype(jnp.bfloat16)
        found.append(lax.dot_general(
            by_row, by_plane, (((1,), (1,)), ((), ())), preferred_element_type=jnp.float32))
    wide_lane = lax.broadcasted_iota(jnp.int32, (64, 128), 1)
    live[...] = jnp.where((wide_lane & 15) < 8, found[0], found[1])

    both = (c, other)
    match((0,), OWN, 1, both)

    q_wait(4)
    q_pass(0, 4, 0, 1)
    q_pass(0, 4, 0, 3)
    q_wait(12)
    q_pass(0, 12, 0, 1)
    q_pass(0, 12, 0, 3)
    q_wait(1)
    q_pass(1, 1, 1, 0)
    q_pass(1, 1, 3, 0)
    q_wait(3)
    q_pass(1, 3, 1, 0)
    q_pass(1, 3, 3, 0)
    z_wait(UP2, 0)
    z_copy(UP2, FAR, 2, 0)
    z_copy(UP2, UP3, 1, 0)
    z_wait(DN2, 1)
    z_copy(DN2, FAR, 6, 1)
    z_copy(DN2, DN3, 7, 1)
    z_wait(UP1)
    share(UP1)
    z_wait(DN1)
    share(DN1)
    q_pass(0, 4, 0, 2)
    q_pass(0, 12, 0, 2)
    q_pass(1, 1, 2, 0)
    q_pass(1, 3, 2, 0)
    q_wait(8)
    q_wait(2)
    for d in (1, 3, 2):
        q_pass(0, 8, 0, d)
        q_pass(1, 2, d, 0)
    match(near, OWN, 1, both)
    inner = near + axis
    match(inner, UP1, 2, (c,))
    z_wait(UP2, 1)
    z_copy(UP2, UP3, 1, 1)
    share(UP2)
    z_wait(DN2, 0)
    z_copy(DN2, DN3, 7, 0)
    share(DN2)
    match(axis, OWN, 1, both)
    match(inner, UP2, 2, (c,))
    share_wait(UP1)
    share_wait(DN1)
    share_wait(UP2)
    share_wait(DN2)
    match(inner, UP1, 4, (other,))

    for s in corner:
        q_wait(s, 0)
        q_wait(s, 1)
    match(corner, OWN, 5, both)
    for part in (0, 1):
        z_wait(UP3, part)
    share(UP3)
    for part in (1, 0):
        z_wait(DN3, part)
    share(DN3)
    for s in far[:2]:
        q_wait(s, 0)
        q_wait(s, 1)
    z_wait(FAR, 0)
    z_wait(FAR, 1)
    share(FAR)
    for s in far[2:]:
        q_wait(s, 0)
        q_wait(s, 1)
    match(far, OWN, 5, both)
    match(range(1, 16), UP3, 3, (c,))
    share_wait(UP3)
    share_wait(DN3)
    share_wait(FAR)

    def deliver(slots):
        for s in slots:
            if s:
                score_copy(s, 0).start()
                score_copy(s, 1).start()

    waves = (far, corner, axis, near)
    for n, wave in enumerate(waves):
        match(wave, UP3, 3, (other,))
        if n:
            sums = [total(s) for s in waves[n - 1]]
            for s, value in zip(waves[n - 1], sums):
                outbox[s] = value
            deliver(waves[n - 1])
    sums = [total(s) for s in waves[-1]]
    for s, value in zip(waves[-1], sums):
        outbox[s] = value
    deliver(waves[-1])

    match((0,), UP1, 7, both)
    own = total(0)
    outbox[0] = own
    inbox[c, 0] = own

    sibling = pltpu.make_async_remote_copy(
        src_ref=outbox.at[0], dst_ref=inbox.at[c, 0], send_sem=ssend.at[0, 0], recv_sem=srecv.at[c, 0],
        device_id={"tok": other}, device_id_type=MESH,
    )
    sibling.start()

    def arrive(tok, slot):
        ref = inbox.at[tok, slot]
        pltpu.make_async_remote_copy(
            src_ref=ref, dst_ref=ref, send_sem=ssend.at[0, 0], recv_sem=srecv.at[tok, slot],
            device_id={"tok": other}, device_id_type=MESH,
        ).wait_recv()

    arrive(other, 0)
    for slot in range(1, 16):
        arrive(0, slot)
        arrive(1, slot)

    regs = []
    for v in range(8):
        pieces = [inbox[0, 2 * v + h] + inbox[1, 2 * v + h] for h in (0, 1)]
        value = jnp.concatenate(pieces, axis=0)
        regs.append(jnp.where(live[v * 8:(v + 1) * 8] > 0.0, value, excluded_score))

    def bit(k):
        return (sub >> (k - 3)) & 1 if k < 6 else (lane >> (k - 2)) & 1

    def partner(value, k):
        if k < 6:
            axis, step, size = 0, 1 << (k - 3), 8
        else:
            axis, step, size = 1, 1 << (k - 2), 128
        if 2 * step == size:
            return pltpu.roll(value, step, axis)
        return jnp.where(bit(k) == 0, pltpu.roll(value, size - step, axis), pltpu.roll(value, step, axis))

    def exchange(regs, k, flips=None):
        if k < 3:
            out = list(regs)
            for v in range(8):
                if v & (1 << k):
                    continue
                u = v | (1 << k)
                high, low = jnp.maximum(regs[v], regs[u]), jnp.minimum(regs[v], regs[u])
                if flips is not None and v & (1 << flips):
                    high, low = low, high
                out[v], out[u] = high, low
            return out
        keep_high = bit(k) == 0
        out = []
        for r in regs:
            mate = partner(r, k)
            out.append(jnp.where(keep_high, jnp.maximum(r, mate), jnp.minimum(r, mate)))
        return out

    def signed(regs, k):
        return [jnp.where(bit(k) == 0, r, -r) for r in regs]

    for phase in range(1, 10):
        top = min(phase - 1, 6)
        if phase in (8, 9):
            regs = [jnp.maximum(r, partner(r, phase - 1)) for r in regs]
        by_mask = 3 <= phase < 9
        if by_mask:
            regs = signed(regs, phase)
        for k in range(top, -1, -1):
            regs = exchange(regs, k, phase if phase < 3 else None)
        if by_mask:
            regs = signed(regs, phase)

    for v in range(8):
        ranked[pl.ds(v, 8, stride=8), :] = regs[v]
    turned = jnp.concatenate([ranked[...], ranked[...]], axis=0).T
    wide = lax.broadcasted_iota(jnp.int32, (16, 128), 1)
    o_ref[...] = jnp.where(wide < 64, turned[0:16], turned[16:32])

    for copy in pending:
        copy.wait_send()
    for slot in range(1, 16):
        score_copy(slot, 0).wait_send()
        score_copy(slot, 1).wait_send()
    sibling.wait_send()


def body(queries, documents, doc_lengths, candidates):
    vmem = pl.BlockSpec(memory_space=pltpu.VMEM)
    return pl.pallas_call(
        kernel,
        out_shape=jax.ShapeDtypeStruct((16, 128), jnp.float32),
        in_specs=[pl.BlockSpec(memory_space=pltpu.HBM)] * 4,
        out_specs=vmem,
        scratch_shapes=[
            pltpu.VMEM((16, 16, 128), jnp.bfloat16),
            pltpu.VMEM((4, 128, 128), jnp.bfloat16),
            pltpu.SMEM((4,), jnp.int32),
            pltpu.VMEM((2, 256), jnp.int32),
            pltpu.SemaphoreType.DMA((4,)),
            pltpu.VMEM((256, 128), jnp.float32),
            pltpu.VMEM((512, 128), jnp.float32),
            pltpu.VMEM((16, 2, 128, 128), jnp.bfloat16),
            pltpu.VMEM((2, 8, 256, 128), jnp.bfloat16),
            pltpu.VMEM((16, 8, 8, 256), jnp.float32),
            pltpu.VMEM((16, 4, 128), jnp.float32),
            pltpu.VMEM((2, 16, 4, 128), jnp.float32),
            pltpu.VMEM((64, 128), jnp.float32),
            pltpu.VMEM((64, 128), jnp.float32),
            pltpu.SemaphoreType.DMA((48,)),
            pltpu.SemaphoreType.DMA((16, 2)),
            pltpu.SemaphoreType.DMA((8, 2)),
            pltpu.SemaphoreType.DMA((8,)),
            pltpu.SemaphoreType.DMA((16, 2)),
            pltpu.SemaphoreType.DMA((2, 16)),
        ],
        compiler_params=pltpu.CompilerParams(
            collective_id=0, has_side_effects=True, vmem_limit_bytes=60 << 20
        ),
    )(queries, documents, doc_lengths, candidates)


def solution(mesh):
    in_specs = (
        P(("query", "doc"), "tok", None),
        P(("query", "doc"), None, None),
        P(("query", "doc")),
        P(("query", "doc"), None),
    )
    out_specs = P(("query", "doc"), None)
    return jax.shard_map(body, mesh=mesh, in_specs=in_specs, out_specs=out_specs, check_vma=False)
```

```python
import jax
import jax.numpy as jnp
from jax import lax
from jax.experimental import pallas as pl
from jax.experimental.pallas import tpu as pltpu
from jax.sharding import PartitionSpec as P

MESH = pl.DeviceIdType.MESH
epsilon = 1e-06
excluded_score = -1e30

OWN, UP1, DN1, UP2, DN2, UP3, DN3, FAR = range(8)
ZOFF = (0, 7, 2, 5, 1, 6, 3, 4)


def unit_rows(values):
    widened = values.astype(jnp.float32)
    return widened * lax.rsqrt(jnp.sum(widened * widened, axis=-1, keepdims=True) + epsilon)


def kernel(
    q_hbm, d_hbm, len_hbm, cand_hbm, o_ref,
    q_ref, d_ref, len_ref, cand_ref, isem, qstage, dstage, qbuf, dbuf, peaks, outbox, inbox, live, ranked,
    qsend, qrecv, drecv, crecv, ssend, srecv,
):
    z = lax.axis_index("query")
    xy = lax.axis_index("doc")
    c = lax.axis_index("tok")
    x, y = xy // 4, xy % 4
    other = 1 - c

    def chip(dx, dy):
        return ((x + dx) % 4) * 4 + (y + dy) % 4

    near = (4, 12, 1, 3)
    axis = (8, 2)
    corner = (5, 7, 13, 15)
    far = (9, 11, 6, 14, 10)
    loads = [
        pltpu.make_async_copy(src, dst, isem.at[n])
        for n, (src, dst) in enumerate(
            ((d_hbm, d_ref), (len_hbm, len_ref), (q_hbm, q_ref), (cand_hbm, cand_ref)))
    ]
    for load in loads:
        load.start()

    barrier = pltpu.get_barrier_semaphore()

    def greet(**place):
        pl.semaphore_signal(barrier, inc=1, device_id=place, device_id_type=MESH)

    for dz in (1, 7, 2, 6):
        greet(query=(z + dz) % 8)
    for slot in near + axis:
        greet(doc=chip(slot // 4, slot % 4))
    greet(tok=other)

    loads[0].wait()
    loads[1].wait()
    slots = lax.broadcasted_iota(jnp.int32, (128, 128), 0)
    for w in range(4):
        unit = unit_rows(d_ref[w])
        unit = jnp.where(slots < len_ref[w], unit, unit[0:1])
        dstage[pl.ds(w, 128, stride=4), :] = unit
    dbuf[:, OWN] = dstage[...].astype(jnp.bfloat16).reshape(2, 256, 128)

    pl.semaphore_wait(barrier, 11)

    pending = []

    def q_copy(ref_from, ref_to, recv, dx, dy):
        copy = pltpu.make_async_remote_copy(
            src_ref=ref_from, dst_ref=ref_to, send_sem=qsend.at[len(pending)], recv_sem=recv,
            device_id={"doc": chip(dx, dy)}, device_id_type=MESH,
        )
        copy.start()
        pending.append(copy)

    def q_send(slot):
        q_copy(qbuf.at[0], qbuf.at[slot], qrecv.at[slot, 0], slot // 4, slot % 4)

    def q_pass(half, slot, dx, dy):
        to = (slot // 4 + dx) % 4 * 4 + (slot % 4 + dy) % 4
        q_copy(qbuf.at[slot, half], qbuf.at[to, half], qrecv.at[to, half], dx, dy)

    def q_wait(slot, half=None):
        ref = qbuf.at[slot] if half is None else qbuf.at[slot, half]
        pltpu.make_async_remote_copy(
            src_ref=ref, dst_ref=ref, send_sem=qsend.at[0], recv_sem=qrecv.at[slot, half or 0],
            device_id={"doc": xy}, device_id_type=MESH,
        ).wait_recv()

    def z_copy(src, chunk, dz, part=None):
        rows = pl.ds(0, 256) if part is None else pl.ds(part * 128, 128)
        copy = pltpu.make_async_remote_copy(
            src_ref=dbuf.at[c, src, rows], dst_ref=dbuf.at[c, chunk, rows], send_sem=qsend.at[len(pending)],
            recv_sem=drecv.at[chunk, part or 0],
            device_id={"query": (z + dz) % 8}, device_id_type=MESH,
        )
        copy.start()
        pending.append(copy)

    def z_wait(chunk, part=None):
        rows = pl.ds(0, 256) if part is None else pl.ds(part * 128, 128)
        ref = dbuf.at[c, chunk, rows]
        pltpu.make_async_remote_copy(
            src_ref=ref, dst_ref=ref, send_sem=qsend.at[0], recv_sem=drecv.at[chunk, part or 0],
            device_id={"query": z}, device_id_type=MESH,
        ).wait_recv()

    def share(chunk):
        copy = pltpu.make_async_remote_copy(
            src_ref=dbuf.at[c, chunk], dst_ref=dbuf.at[c, chunk], send_sem=qsend.at[len(pending)],
            recv_sem=crecv.at[chunk], device_id={"tok": other}, device_id_type=MESH,
        )
        copy.start()
        pending.append(copy)

    def share_wait(chunk):
        ref = dbuf.at[other, chunk]
        pltpu.make_async_remote_copy(
            src_ref=ref, dst_ref=ref, send_sem=qsend.at[0], recv_sem=crecv.at[chunk],
            device_id={"tok": c}, device_id_type=MESH,
        ).wait_recv()

    def match(slots, start, count, halves):
        for half in halves:
            joins = half is other
            for slot in slots:
                similar = lax.dot_general(
                    dbuf[half, start:start + count].reshape(count * 256, 128), qbuf[slot].reshape(256, 128),
                    (((1,), (1,)), ((), ())), preferred_element_type=jnp.float32,
                )
                best = jnp.max(similar.reshape(count, 32, 8, 256), axis=1)
                if joins:
                    best = jnp.maximum(best, peaks[slot, start:start + count])
                peaks[slot, start:start + count] = best

    sub = lax.broadcasted_iota(jnp.int32, (8, 128), 0)
    lane = lax.broadcasted_iota(jnp.int32, (8, 128), 1)

    def total(slot):
        pairs = []
        for p in range(4):
            both = 0.0
            for h in range(2):
                a = peaks[slot, 2 * p, :, h * 128:(h + 1) * 128]
                b = peaks[slot, 2 * p + 1, :, h * 128:(h + 1) * 128]
                first = jnp.where(sub < 4, a, b)
                second = jnp.where(sub < 4, b, a)
                both = both + jnp.maximum(first, pltpu.roll(second, 4, 0))
            pairs.append(both)
        low = lane < 64
        folded = []
        for p in (0, 2):
            a, b = pairs[p], pairs[p + 1]
            folded.append(jnp.where(low, a, b) + pltpu.roll(jnp.where(low, b, a), 64, 1))
        f0, f1 = folded
        quarter = jnp.where((lane & 63) < 32, f0 + pltpu.roll(f0, 96, 1), f1 + pltpu.roll(f1, 32, 1))
        even = quarter + pltpu.roll(quarter, 112, 1)
        odd = quarter + pltpu.roll(quarter, 16, 1)
        return jnp.where((lane & 31) < 16, even, pltpu.roll(odd, 4, 0))[0:4]

    def score_copy(slot, tok):
        return pltpu.make_async_remote_copy(
            src_ref=outbox.at[slot], dst_ref=inbox.at[c, slot], send_sem=ssend.at[slot, tok],
            recv_sem=srecv.at[c, slot],
            device_id={"doc": ((x - slot // 4 + 4) % 4) * 4 + (y - slot % 4 + 4) % 4, "tok": tok},
            device_id_type=MESH,
        )

    z_copy(OWN, UP2, 2, 0)
    z_copy(OWN, DN2, 6, 1)
    z_copy(OWN, UP1, 1)
    z_copy(OWN, DN1, 7)

    loads[2].wait()
    unit = unit_rows(q_ref[...]).reshape(256, 128)
    for n in range(16):
        qstage[pl.ds(n, 16, stride=16), :] = unit[n * 16:(n + 1) * 16]
    qbuf[0] = qstage[...].astype(jnp.bfloat16).reshape(2, 128, 128)
    for slot in near + axis:
        q_send(slot)
    z_copy(OWN, UP2, 2, 1)
    z_copy(OWN, DN2, 6, 0)
    loads[3].wait()

    rows = lax.broadcasted_iota(jnp.int32, (64, 256), 0)
    source = rows >> 2
    row_id = (((x + (source >> 2)) & 3) * 4 + ((y + source) & 3)) * 4 + (rows & 3)
    lanes = lax.broadcasted_iota(jnp.int32, (128, 256), 0)
    group = lanes >> 4
    plane = jnp.zeros_like(group)
    for g in range(8):
        plane = jnp.where(group == g, (z + ZOFF[g]) % 8, plane)
    first = cand_ref[0:1, :]
    second = cand_ref[1:2, :]
    listed = jnp.where((lanes & 15) < 8, first, second)
    by_plane = jnp.where(listed >> 6 == plane, 1.0, 0.0).astype(jnp.bfloat16)
    found = []
    for block in (first, second):
        by_row = jnp.where(block & 63 == row_id, 1.0, 0.0).astype(jnp.bfloat16)
        found.append(lax.dot_general(
            by_row, by_plane, (((1,), (1,)), ((), ())), preferred_element_type=jnp.float32))
    wide_lane = lax.broadcasted_iota(jnp.int32, (64, 128), 1)
    live[...] = jnp.where((wide_lane & 15) < 8, found[0], found[1])

    both = (c, other)
    match((0,), OWN, 1, both)

    q_wait(4)
    q_pass(0, 4, 0, 1)
    q_pass(0, 4, 0, 3)
    q_wait(12)
    q_pass(0, 12, 0, 1)
    q_pass(0, 12, 0, 3)
    q_wait(1)
    q_pass(1, 1, 1, 0)
    q_pass(1, 1, 3, 0)
    q_wait(3)
    q_pass(1, 3, 1, 0)
    q_pass(1, 3, 3, 0)
    z_wait(UP2, 0)
    z_copy(UP2, FAR, 2, 0)
    z_copy(UP2, UP3, 1, 0)
    z_wait(DN2, 1)
    z_copy(DN2, FAR, 6, 1)
    z_copy(DN2, DN3, 7, 1)
    z_wait(UP1)
    share(UP1)
    z_wait(DN1)
    share(DN1)
    q_pass(0, 4, 0, 2)
    q_pass(0, 12, 0, 2)
    q_pass(1, 1, 2, 0)
    q_pass(1, 3, 2, 0)
    q_wait(8)
    q_wait(2)
    for d in (1, 3, 2):
        q_pass(0, 8, 0, d)
        q_pass(1, 2, d, 0)
    match(near, OWN, 1, both)
    inner = near + axis
    match(inner, UP1, 2, (c,))
    z_wait(UP2, 1)
    z_copy(UP2, UP3, 1, 1)
    share(UP2)
    z_wait(DN2, 0)
    z_copy(DN2, DN3, 7, 0)
    share(DN2)
    match(axis, OWN, 1, both)
    match(inner, UP2, 2, (c,))
    share_wait(UP1)
    share_wait(DN1)
    share_wait(UP2)
    share_wait(DN2)
    match(inner, UP1, 4, (other,))

    for s in corner:
        q_wait(s, 0)
        q_wait(s, 1)
    match(corner, OWN, 5, both)
    for part in (0, 1):
        z_wait(UP3, part)
    share(UP3)
    for part in (1, 0):
        z_wait(DN3, part)
    share(DN3)
    match(inner + corner, UP3, 2, (c,))
    for s in far:
        q_wait(s, 0)
        q_wait(s, 1)
    z_wait(FAR, 0)
    z_wait(FAR, 1)
    share(FAR)
    match(far, OWN, 5, both)
    match(far, UP3, 3, (c,))
    match(inner + corner, FAR, 1, (c,))
    share_wait(UP3)
    share_wait(DN3)
    share_wait(FAR)

    def deliver(slots):
        for s in slots:
            if s:
                score_copy(s, 0).start()
                score_copy(s, 1).start()

    waves = (far, corner, axis, near)
    for n, wave in enumerate(waves):
        match(wave, UP3, 3, (other,))
        if n:
            sums = [total(s) for s in waves[n - 1]]
            for s, value in zip(waves[n - 1], sums):
                outbox[s] = value
            deliver(waves[n - 1])
    sums = [total(s) for s in waves[-1]]
    for s, value in zip(waves[-1], sums):
        outbox[s] = value
    deliver(waves[-1])

    match((0,), UP1, 7, both)
    own = total(0)
    outbox[0] = own
    inbox[c, 0] = own

    sibling = pltpu.make_async_remote_copy(
        src_ref=outbox.at[0], dst_ref=inbox.at[c, 0], send_sem=ssend.at[0, 0], recv_sem=srecv.at[c, 0],
        device_id={"tok": other}, device_id_type=MESH,
    )
    sibling.start()

    def arrive(tok, slot):
        ref = inbox.at[tok, slot]
        pltpu.make_async_remote_copy(
            src_ref=ref, dst_ref=ref, send_sem=ssend.at[0, 0], recv_sem=srecv.at[tok, slot],
            device_id={"tok": other}, device_id_type=MESH,
        ).wait_recv()

    arrive(other, 0)
    for slot in range(1, 16):
        arrive(0, slot)
        arrive(1, slot)

    regs = []
    for v in range(8):
        pieces = [inbox[0, 2 * v + h] + inbox[1, 2 * v + h] for h in (0, 1)]
        value = jnp.concatenate(pieces, axis=0)
        regs.append(jnp.where(live[v * 8:(v + 1) * 8] > 0.0, value, excluded_score))

    def bit(k):
        return (sub >> (k - 3)) & 1 if k < 6 else (lane >> (k - 2)) & 1

    def partner(value, k):
        if k < 6:
            axis, step, size = 0, 1 << (k - 3), 8
        else:
            axis, step, size = 1, 1 << (k - 2), 128
        if 2 * step == size:
            return pltpu.roll(value, step, axis)
        return jnp.where(bit(k) == 0, pltpu.roll(value, size - step, axis), pltpu.roll(value, step, axis))

    def exchange(regs, k, flips=None):
        if k < 3:
            out = list(regs)
            for v in range(8):
                if v & (1 << k):
                    continue
                u = v | (1 << k)
                high, low = jnp.maximum(regs[v], regs[u]), jnp.minimum(regs[v], regs[u])
                if flips is not None and v & (1 << flips):
                    high, low = low, high
                out[v], out[u] = high, low
            return out
        keep_high = bit(k) == 0
        out = []
        for r in regs:
            mate = partner(r, k)
            out.append(jnp.where(keep_high, jnp.maximum(r, mate), jnp.minimum(r, mate)))
        return out

    def signed(regs, k):
        return [jnp.where(bit(k) == 0, r, -r) for r in regs]

    for phase in range(1, 10):
        top = min(phase - 1, 6)
        if phase in (8, 9):
            regs = [jnp.maximum(r, partner(r, phase - 1)) for r in regs]
        by_mask = 3 <= phase < 9
        if by_mask:
            regs = signed(regs, phase)
        for k in range(top, -1, -1):
            regs = exchange(regs, k, phase if phase < 3 else None)
        if by_mask:
            regs = signed(regs, phase)

    for v in range(8):
        ranked[pl.ds(v, 8, stride=8), :] = regs[v]
    turned = jnp.concatenate([ranked[...], ranked[...]], axis=0).T
    wide = lax.broadcasted_iota(jnp.int32, (16, 128), 1)
    o_ref[...] = jnp.where(wide < 64, turned[0:16], turned[16:32])

    for copy in pending:
        copy.wait_send()
    for slot in range(1, 16):
        score_copy(slot, 0).wait_send()
        score_copy(slot, 1).wait_send()
    sibling.wait_send()


def body(queries, documents, doc_lengths, candidates):
    vmem = pl.BlockSpec(memory_space=pltpu.VMEM)
    return pl.pallas_call(
        kernel,
        out_shape=jax.ShapeDtypeStruct((16, 128), jnp.float32),
        in_specs=[pl.BlockSpec(memory_space=pltpu.HBM)] * 4,
        out_specs=vmem,
        scratch_shapes=[
            pltpu.VMEM((16, 16, 128), jnp.bfloat16),
            pltpu.VMEM((4, 128, 128), jnp.bfloat16),
            pltpu.SMEM((4,), jnp.int32),
            pltpu.VMEM((2, 256), jnp.int32),
            pltpu.SemaphoreType.DMA((4,)),
            pltpu.VMEM((256, 128), jnp.float32),
            pltpu.VMEM((512, 128), jnp.float32),
            pltpu.VMEM((16, 2, 128, 128), jnp.bfloat16),
            pltpu.VMEM((2, 8, 256, 128), jnp.bfloat16),
            pltpu.VMEM((16, 8, 8, 256), jnp.float32),
            pltpu.VMEM((16, 4, 128), jnp.float32),
            pltpu.VMEM((2, 16, 4, 128), jnp.float32),
            pltpu.VMEM((64, 128), jnp.float32),
            pltpu.VMEM((64, 128), jnp.float32),
            pltpu.SemaphoreType.DMA((48,)),
            pltpu.SemaphoreType.DMA((16, 2)),
            pltpu.SemaphoreType.DMA((8, 2)),
            pltpu.SemaphoreType.DMA((8,)),
            pltpu.SemaphoreType.DMA((16, 2)),
            pltpu.SemaphoreType.DMA((2, 16)),
        ],
        compiler_params=pltpu.CompilerParams(
            collective_id=0, has_side_effects=True, vmem_limit_bytes=60 << 20
        ),
    )(queries, documents, doc_lengths, candidates)


def solution(mesh):
    in_specs = (
        P(("query", "doc"), "tok", None),
        P(("query", "doc"), None, None),
        P(("query", "doc")),
        P(("query", "doc"), None),
    )
    out_specs = P(("query", "doc"), None)
    return jax.shard_map(body, mesh=mesh, in_specs=in_specs, out_specs=out_specs, check_vma=False)
```
